32 devices in a mesh: dp: 4 (over y, x), exp: 8 (over z, core).
Axes of the slice: x: 2, y: 2, z: 4, core: 2. Of those that a mesh axis runs over, the one named last changes fastest.
Arguments:
- hidden: bfloat16 [4096, 2048], P(('dp', 'exp')), may hold values from -6 to 6
- queries: bfloat16 [4096, 2048], P(('dp', 'exp')), may hold values from -1000 to 1000
- draft_entries: bfloat16 [2, 4096, 512], P(None, ('dp', 'exp')), may hold values from -6 to 6
- key_pool: bfloat16 [256, 64, 512], P(('dp', 'exp')), may hold values from -8 to 8
- value_pool: bfloat16 [256, 64, 512], P(('dp', 'exp')), may hold values from -6 to 6
- page_table: int32 [64, 4], P(('dp', 'exp')), may hold values from 0 to 31, as said below
- cache_len: int32 [64], P(('dp', 'exp')), may hold values from 2 to 256, as said below
- parents: int32 [64, 64], P(('dp', 'exp')), may hold values from -1 to 62, as said below
- out_proj: bfloat16 [2048, 2048], replicated, may hold values from -0.125 to 0.125
- norm_gain: bfloat16 [2048], replicated, may hold values from 0.099609375 to 1.8984375
- expert_gate: bfloat16 [64, 1408, 2048], P('exp', 'dp'), may hold values from -0.125 to 0.125
- expert_up: bfloat16 [64, 1408, 2048], P('exp', 'dp'), may hold values from -0.125 to 0.125
- expert_down: bfloat16 [64, 1408, 2048], P('exp', 'dp'), may hold values from -0.15625 to 0.15625
- shared_gate: bfloat16 [1408, 2048], P('dp'), may hold values from -0.125 to 0.125
- shared_up: bfloat16 [1408, 2048], P('dp'), may hold values from -0.125 to 0.125
- shared_down: bfloat16 [1408, 2048], P('dp'), may hold values from -0.15625 to 0.15625
- expert_ids: int32 [4096, 6], P(('dp', 'exp')), may hold values from 0 to 63, all different within a row; in each aligned block of 128 rows (0 to 127, 128 to 255, ...) at most 16 rows name the same one
- expert_weights: float32 [4096, 6], P(('dp', 'exp')), may hold values from 0.05 to 0.5
Outputs:
- verified: bfloat16 [4096, 2048], P(('dp', 'exp'))
The draws below stay inside these ranges and needn't reach their ends.
Inputs may be any that keep to these rules, and one draw needn't show every extreme that they name: `page_table`: page ids count within the 4 devices that share the request's index of exp: page q lies on the one of dp index q // 8, as its page q % 8; the requests of those devices together use each of their 32 pages exactly once. `cache_len`: some request has exactly 256 cached positions. parents[r, i] is -1 or an earlier node i' < i of the same request; parents[r, 0] = -1. `expert_ids`: each row names 6 different experts; the 128 rows of one device name one expert at most 16 times, a bound that some block reaches.
All inputs are finite; a program needn't handle non-finite values.
Results may differ from the reference program's by a relative error of at most 0.015.
Values may be sent and summed in bfloat16 or wider, within the bound.
A program may use at most 192 MiB of HBM per device.

```python
import math
import jax
import jax.numpy as jnp
import numpy as np
from jax import lax

D = 2048
HEADS = 16
KVH = 4
HD = 128
EXPERTS = 64
FF = 1408
TOP = 6
SHFF = 1408
REQ_DEV = 2
DRAFT = 64
PAGE = 64
MAXPG = 4
CAP = 16
DP_SPAN = 4
EXP_SPAN = 8
REQUESTS = 64
TOKENS = 4096
TOK_DEV = 128
POOL = 8
GROUP_PAGES = 32
PAGES = 256
CMAX = 256
QW = 2048
KW = 512
FF_PART = 352
SH_PART = 352


def group_pages(key):
    ordered = jnp.tile(jnp.arange(GROUP_PAGES, dtype=jnp.int32)[None, :], (EXP_SPAN, 1))
    mixed = jax.random.permutation(jax.random.fold_in(key, 7), ordered, axis=1, independent=True)
    mixed = mixed.reshape(EXP_SPAN, DP_SPAN, REQ_DEV, MAXPG)
    return jnp.transpose(mixed, (1, 0, 2, 3)).reshape(REQUESTS, MAXPG).astype(jnp.int32)


def pool_first(key):
    return jax.random.normal(jax.random.fold_in(key, 11), (PAGES, 1, KW), jnp.float32)


def draw_page_table(key, part):
    return group_pages(key)


def draw_key_pool(key, part):
    opening_keys = pool_first(key)
    remaining = jax.random.normal(jax.random.fold_in(key, 14), (PAGES, PAGE - 1, KW), jnp.float32)
    return jnp.concatenate([opening_keys, remaining], axis=1).astype(jnp.bfloat16)


def draw_queries(key, part):
    values = jax.random.normal(jax.random.fold_in(key, 13), (TOKENS, QW), jnp.float32)
    return values.astype(jnp.bfloat16)


def draw_cache_len(key, part):
    lengths = jax.random.randint(jax.random.fold_in(key, 21), (REQUESTS,), 2, CMAX + 1)
    longest = jax.random.randint(jax.random.fold_in(key, 22), (), 0, REQUESTS)
    return jnp.where(jnp.arange(REQUESTS) == longest, CMAX, lengths).astype(jnp.int32)


def draw_parents(key, part):
    raw_bits = jax.random.randint(jax.random.fold_in(key, 31), (REQUESTS, DRAFT), 0, 1 << 20)
    node_index = jnp.arange(DRAFT, dtype=jnp.int32)
    linked = raw_bits % (node_index + 1)[None, :] - 1
    forced = (jnp.arange(REQUESTS)[:, None] == 0) & (node_index[None, :] == DRAFT - 1)
    return jnp.where(forced, DRAFT - 2, linked).astype(jnp.int32)


def level_of(rng, shape, pieces, least, top_value):
    factor_of, own = 1.0, jax.random.fold_in(rng, 6)
    for position, blocks in pieces:
        heights = jnp.exp(jax.random.uniform(jax.random.fold_in(own, position), (blocks,), jnp.float32, least / len(pieces), top_value / len(pieces)))
        factor_of = factor_of * jnp.repeat(heights, shape[position] // blocks).reshape([-1 if axis == position else 1 for axis in range(len(shape))])
    return factor_of


def deal_out(rng, own, number, rows, number_of, top, reach, slope):
    ranking = jax.random.permutation(rng, number_of)
    heavy_load, ordinary = load_shares(number_of, rows * top, reach, slope, True), load_shares(number_of, rows * top, reach, slope, False)
    places = jnp.arange(number_of)

    def named(tallies, offset_by):
        used = int((tallies > 0).sum())
        fixed = max(1, used // 4)
        passed = fixed + (places - fixed + offset_by * (used - fixed)) % max(1, number_of - fixed)
        return jnp.zeros((number_of,), jnp.int32).at[ranking[jnp.where(places < fixed, places, passed)]].set(jnp.asarray(tallies, jnp.int32))

    tallies = jnp.where(number % 4 == 0, named(heavy_load, number // 4), named(ordinary, number - number // 4 - 1))
    mixed = jax.random.permutation(jax.random.fold_in(own, 3), number_of)
    giver, taker = mixed[0:number_of // 2 * 2:2], mixed[1:number_of // 2 * 2:2]
    room = jnp.minimum(tallies[giver] - 1, reach - tallies[taker]) // 2
    room = jnp.where((giver == ranking[0]) | (taker == ranking[0]) | (tallies[taker] == 0), 0, jnp.maximum(room, 0))
    passed = jax.random.randint(jax.random.fold_in(own, 4), (number_of // 2,), 0, 1 << 20) % (room + 1)
    tallies = tallies.at[giver].add(-passed).at[taker].add(passed)
    members = jnp.searchsorted(jnp.cumsum(tallies), jnp.arange(rows * top), side="right").astype(jnp.int32)
    grid = members.reshape(top, rows).T
    grid = grid[jax.random.permutation(jax.random.fold_in(own, 1), rows)]
    offset_by = jax.random.randint(jax.random.fold_in(own, 2), (rows, 1), 0, top)
    return jnp.take_along_axis(grid, (jnp.arange(top)[None, :] + offset_by) % top, axis=1)


def load_shares(count, total, most, lean, full):
    weights = [(1 << 20) // math.isqrt(standing ** lean) + 1 for standing in range(1, count + 1)]
    largest = most if full else min(most, max(-(-total // count), total * weights[0] // sum(weights)))
    least = 1 if total - largest >= count - 1 else 0
    given, rest = [largest] + [least] * (count - 1), total - largest - least * (count - 1)
    while rest > 0:
        free = [i for i in range(1, count) if given[i] < largest] or [i for i in range(1, count) if given[i] < most]
        mass, left = sum([weights[i] for i in free]), rest
        for i in free:
            more = min(most - given[i], max(1, left * weights[i] // mass), rest)
            given[i] = given[i] + more
            rest = rest - more
    return np.array(given)


def scatter_about(rng, shape, scale, bound, pieces=(), kind=jnp.bfloat16):
    entries = scale * jax.random.normal(rng, shape, jnp.float32)
    if pieces:
        entries = entries * level_of(rng, shape, pieces, -0.22, 0.18)
    return jnp.clip(entries, -bound, bound).astype(kind)


def setup_inputs(seed: int = 0) -> dict:
    key_list = jax.random.split(jax.random.key(seed), 19)
    hidden = scatter_about(key_list[0], (TOKENS, D), 1.0, 6.0, ((0, 32),))
    queries = draw_queries(jax.random.fold_in(key_list[18], 71), 0)
    draft_entries = scatter_about(key_list[2], (2, TOKENS, KW), 1.0, 6.0, ((1, 32),))
    key_pool = draw_key_pool(jax.random.fold_in(key_list[18], 71), 0)
    value_pool = scatter_about(key_list[4], (PAGES, PAGE, KW), 1.0, 6.0, ((0, 32),))
    page_table = draw_page_table(jax.random.fold_in(key_list[18], 71), 0)
    cache_len = draw_cache_len(jax.random.fold_in(key_list[18], 71), 0)
    parents = draw_parents(jax.random.fold_in(key_list[18], 71), 0)
    out_proj = scatter_about(key_list[8], (QW, D), QW ** -0.5, 0.125)
    norm_gain = jnp.clip(1.0 + 0.18 * jax.random.normal(key_list[9], (D,), jnp.float32), 0.099609375, 1.8984375).astype(jnp.bfloat16)
    expert_gate = scatter_about(key_list[10], (EXPERTS, FF, D), D ** -0.5, 0.125, ((0, 8), (1, 4)))
    expert_up = scatter_about(key_list[11], (EXPERTS, FF, D), D ** -0.5, 0.125, ((0, 8), (1, 4)))
    expert_down = scatter_about(key_list[12], (EXPERTS, FF, D), FF ** -0.5, 0.15625, ((0, 8), (1, 4)))
    shared_gate = scatter_about(key_list[13], (SHFF, D), D ** -0.5, 0.125, ((0, 4),))
    shared_up = scatter_about(key_list[14], (SHFF, D), D ** -0.5, 0.125, ((0, 4),))
    shared_down = scatter_about(key_list[15], (SHFF, D), SHFF ** -0.5, 0.15625, ((0, 4),))
    expert_ids_keys = jax.random.split(jax.random.fold_in(key_list[16], 1), TOKENS // TOK_DEV)
    expert_ids_turns = jax.random.permutation(jax.random.fold_in(key_list[16], 3), TOKENS // TOK_DEV)
    expert_ids = jax.vmap(lambda own, number: deal_out(jax.random.fold_in(key_list[16], 2), own, number, TOK_DEV, EXPERTS, TOP, CAP, 2))(expert_ids_keys, expert_ids_turns).reshape((TOKENS, TOP))
    expert_weights = jnp.clip(jnp.exp(math.log(0.5) - 2.3025851 * jax.random.uniform(key_list[17], (TOKENS, TOP), jnp.float32) ** level_of(key_list[17], (TOKENS, TOP), ((0, 32),), -0.2, 0.2)), 0.05, 0.5)
    return {"hidden": hidden, "queries": queries, "draft_entries": draft_entries, "key_pool": key_pool, "value_pool": value_pool, "page_table": page_table, "cache_len": cache_len, "parents": parents, "out_proj": out_proj, "norm_gain": norm_gain, "expert_gate": expert_gate, "expert_up": expert_up, "expert_down": expert_down, "shared_gate": shared_gate, "shared_up": shared_up, "shared_down": shared_down, "expert_ids": expert_ids, "expert_weights": expert_weights}


NEG_FILL = -1e+30
NORM_EPSILON = 1e-06
HIGHEST_PRECISION = lax.Precision.HIGHEST

def tree_reach(parents):
    node_count = parents.shape[-1]
    node_index = jnp.arange(node_count, dtype=jnp.int32)
    linked = (parents[:, :, None] == node_index[None, None, :]).astype(jnp.float32)
    reached = jnp.minimum(linked + jnp.eye(node_count, dtype=jnp.float32)[None], 1.0)
    for rounds in range(max(1, (node_count - 1).bit_length())):
        reached = jnp.minimum(jnp.einsum('rij,rjk->rik', reached, reached, precision=HIGHEST_PRECISION), 1.0)
    return reached

def reference(hidden, queries, draft_entries, key_pool, value_pool, page_table, cache_len, parents, out_proj, norm_gain, expert_gate, expert_up, expert_down, shared_gate, shared_up, shared_down, expert_ids, expert_weights):
    group_size = HEADS // KVH
    reached = tree_reach(parents)
    request_index = jnp.arange(REQUESTS, dtype=jnp.int32)
    columns = request_index // REQ_DEV % EXP_SPAN
    page_index = page_table // POOL * (EXP_SPAN * POOL) + columns[:, None] * POOL + page_table % POOL
    positions = jnp.arange(CMAX, dtype=jnp.int32)

    def attend(items):
        query_rows, draft_keys, draft_values, page_rows, cache_size, reach_rows = items
        cache_keys = key_pool[page_rows].reshape(CMAX, KW)
        cache_values = value_pool[page_rows].reshape(CMAX, KW)
        all_keys = jnp.concatenate([cache_keys, draft_keys], axis=0).astype(jnp.float32).reshape(CMAX + DRAFT, KVH, HD)
        all_values = jnp.concatenate([cache_values, draft_values], axis=0).astype(jnp.float32).reshape(CMAX + DRAFT, KVH, HD)
        query_heads = query_rows.astype(jnp.float32).reshape(DRAFT, KVH, group_size, HD)
        scores = jnp.einsum('tgnd,cgd->gntc', query_heads, all_keys) * HD ** (-0.5)
        cache_live = jnp.broadcast_to(positions[None, :] < cache_size, (DRAFT, CMAX))
        live_mask = jnp.concatenate([cache_live, reach_rows > 0.5], axis=1)
        scores = jnp.where(live_mask[None, None], scores, NEG_FILL)
        row_top = lax.optimization_barrier(jnp.max(scores, axis=-1, keepdims=True))
        exponents = jnp.where(live_mask[None, None], jnp.exp(scores - row_top), 0.0)
        totals = lax.optimization_barrier(jnp.sum(exponents, axis=-1))
        weights = lax.optimization_barrier(exponents.astype(jnp.bfloat16)).astype(jnp.float32)
        mixed = jnp.einsum('gntc,cgd->tgnd', weights, all_values)
        mixed = mixed / jnp.transpose(totals, (2, 0, 1))[..., None]
        return mixed.reshape(DRAFT, QW).astype(jnp.bfloat16)
    attention = lax.map(attend, (queries.reshape(REQUESTS, DRAFT, QW), draft_entries[0].reshape(REQUESTS, DRAFT, KW), draft_entries[1].reshape(REQUESTS, DRAFT, KW), page_index, cache_len, reached))
    attention = attention.reshape(TOKENS, QW)
    residual = (hidden.astype(jnp.float32) + jnp.dot(attention, out_proj, preferred_element_type=jnp.float32)).astype(jnp.bfloat16)
    residual_wide = residual.astype(jnp.float32)
    scale_rows = lax.rsqrt(lax.optimization_barrier(jnp.mean(residual_wide * residual_wide, axis=-1, keepdims=True)) + NORM_EPSILON)
    normed = (residual_wide * scale_rows * norm_gain.astype(jnp.float32)).astype(jnp.bfloat16)
    block_count = TOKENS // TOK_DEV
    block_rows = TOK_DEV * TOP
    flat_experts = expert_ids.reshape(block_count, block_rows)
    expert_range = jnp.arange(EXPERTS, dtype=jnp.int32)
    onehot = (flat_experts[:, :, None] == expert_range[None, None, :]).astype(jnp.int32)
    slot_index = lax.optimization_barrier(jnp.sum((jnp.cumsum(onehot, axis=1) - 1) * onehot, axis=2))
    block_index = jnp.arange(block_count, dtype=jnp.int32)[:, None]
    destinations = flat_experts * (block_count * CAP) + block_index * CAP + slot_index
    token_index = block_index * TOK_DEV + jnp.arange(block_rows, dtype=jnp.int32)[None, :] // TOP
    slot_count = EXPERTS * block_count * CAP
    source_rows = jnp.full((slot_count,), TOKENS, jnp.int32).at[destinations.reshape(-1)].set(token_index.reshape(-1))
    slot_weights = jnp.zeros((slot_count,), jnp.float32).at[destinations.reshape(-1)].set(expert_weights.reshape(-1))
    source_rows = source_rows.reshape(EXPERTS, block_count * CAP)
    slot_weights = slot_weights.reshape(EXPERTS, block_count * CAP)
    padded = jnp.concatenate([normed, jnp.zeros((1, D), jnp.bfloat16)], axis=0)

    def one_expert(running, items):
        row_index, row_weights, gate_rows, upper_rows, down_rows = items
        inputs = padded[row_index].astype(jnp.float32)
        gate_values = jnp.einsum('rd,fd->rf', inputs, gate_rows.astype(jnp.float32))
        upper_values = jnp.einsum('rd,fd->rf', inputs, upper_rows.astype(jnp.float32))
        inner = lax.optimization_barrier((jax.nn.silu(gate_values) * upper_values).astype(jnp.bfloat16)).astype(jnp.float32)
        part_terms = jnp.einsum('rqf,qfd->rqd', inner.reshape(-1, DP_SPAN, FF_PART), down_rows.astype(jnp.float32).reshape(DP_SPAN, FF_PART, D))
        part_terms = lax.optimization_barrier(part_terms.astype(jnp.bfloat16)).astype(jnp.float32)
        expert_out = lax.optimization_barrier(lax.optimization_barrier(jnp.sum(part_terms, axis=1)).astype(jnp.bfloat16)).astype(jnp.float32)
        return (running.at[row_index].add(expert_out * row_weights[:, None], mode='drop'), None)
    routed, unused = lax.scan(one_expert, jnp.zeros((TOKENS, D), jnp.float32), (source_rows, slot_weights, expert_gate, expert_up, expert_down))
    shared_sum = jnp.zeros((TOKENS, D), jnp.float32)
    for section in range(DP_SPAN):
        first_unit = section * SH_PART
        gate_values = jnp.dot(normed, shared_gate[first_unit:first_unit + SH_PART].T, preferred_element_type=jnp.float32)
        upper_values = jnp.dot(normed, shared_up[first_unit:first_unit + SH_PART].T, preferred_element_type=jnp.float32)
        shared_inner = (jax.nn.silu(gate_values) * upper_values).astype(jnp.bfloat16)
        shared_term = jnp.dot(shared_inner, shared_down[first_unit:first_unit + SH_PART], preferred_element_type=jnp.float32).astype(jnp.bfloat16)
        shared_sum = shared_sum + shared_term.astype(jnp.float32)
    return (residual.astype(jnp.float32) + routed + shared_sum).astype(jnp.bfloat16)
```

```python
import jax
import jax.numpy as jnp
from jax import lax
from jax.experimental import pallas as pl
from jax.experimental.pallas import tpu as pltpu
from jax.sharding import PartitionSpec as P

HEADS = 16
KVH = 4
HD = 128
CAP = 16


NEG_FILL = -1e30
NORM_EPSILON = 1e-06
HIGHEST_PRECISION = lax.Precision.HIGHEST


def tree_reach(parents):
    node_count = parents.shape[-1]
    node_index = jnp.arange(node_count, dtype=jnp.int32)
    linked = (parents[:, :, None] == node_index[None, None, :]).astype(jnp.float32)
    reached = jnp.minimum(linked + jnp.eye(node_count, dtype=jnp.float32)[None], 1.0)
    for rounds in range(max(1, (node_count - 1).bit_length())):
        reached = jnp.minimum(
            jnp.einsum("rij,rjk->rik", reached, reached, precision=HIGHEST_PRECISION), 1.0
        )
    return reached


def score_block(query_heads, key_rows, live_mask):
    raw_scores = jnp.einsum(
        "rtgnd,rcgd->rgntc", query_heads, key_rows, preferred_element_type=jnp.float32
    ) * key_rows.shape[-1] ** (-0.5)
    wide_mask = live_mask[:, None, None]
    return (jnp.where(wide_mask, raw_scores, NEG_FILL), wide_mask)


def fold_keys(carry_state, scores, wide_mask, value_rows):
    running_top, running_total, running_sum = carry_state
    fresh_top = jnp.maximum(running_top, jnp.max(scores, axis=-1))
    rescale = jnp.exp(running_top - fresh_top)
    exponents = jnp.where(wide_mask, jnp.exp(scores - fresh_top[..., None]), 0.0)
    weights = exponents.astype(jnp.bfloat16)
    new_total = running_total * rescale + jnp.sum(exponents, axis=-1)
    mixed = jnp.einsum("rgntc,rcgd->rtgnd", weights, value_rows, preferred_element_type=jnp.float32)
    new_sum = running_sum * jnp.transpose(rescale, (0, 3, 1, 2))[..., None] + mixed
    return (fresh_top, new_total, new_sum)


def pool_state(carry_state, query_heads, table_rows, lengths, pieces):
    piece_keys, piece_values = pieces
    piece_count = piece_keys.shape[0]
    request_count, pages_per = table_rows.shape
    page_size = piece_keys.shape[1]
    key_heads = query_heads.shape[2]
    inside = (table_rows >= 0) & (table_rows < piece_count)
    picked = jnp.clip(table_rows, 0, piece_count - 1)
    cache_keys = piece_keys[picked].reshape(request_count, pages_per * page_size, key_heads, -1)
    cache_values = piece_values[picked].reshape(request_count, pages_per * page_size, key_heads, -1)
    positions = jnp.arange(pages_per * page_size, dtype=jnp.int32)
    usable = jnp.repeat(inside, page_size, axis=1) & (positions[None, :] < lengths[:, None])
    live_mask = jnp.broadcast_to(
        usable[:, None, :], (request_count, query_heads.shape[1], pages_per * page_size)
    )
    scores, wide_mask = score_block(query_heads, cache_keys, live_mask)
    return fold_keys(carry_state, scores, wide_mask, cache_values)


def blank_state(request_count, draft_nodes, key_heads, group_size, head_size):
    return (
        jnp.full((request_count, key_heads, group_size, draft_nodes), NEG_FILL, jnp.float32),
        jnp.zeros((request_count, key_heads, group_size, draft_nodes), jnp.float32),
        jnp.zeros((request_count, draft_nodes, key_heads, group_size, head_size), jnp.float32),
    )


def expert_block(grouped, gate_rows, upper_rows, down_rows):
    gate_values = jnp.einsum(
        "sekd,efd->sekf", grouped, gate_rows, preferred_element_type=jnp.float32
    )
    upper_values = jnp.einsum(
        "sekd,efd->sekf", grouped, upper_rows, preferred_element_type=jnp.float32
    )
    inner = (jax.nn.silu(gate_values) * upper_values).astype(jnp.bfloat16)
    return jnp.einsum("sekf,efd->sekd", inner, down_rows, preferred_element_type=jnp.float32)


def shared_block(tokens, gate_rows, upper_rows, down_rows):
    gate_values = jnp.einsum("td,fd->tf", tokens, gate_rows, preferred_element_type=jnp.float32)
    upper_values = jnp.einsum("td,fd->tf", tokens, upper_rows, preferred_element_type=jnp.float32)
    inner = (jax.nn.silu(gate_values) * upper_values).astype(jnp.bfloat16)
    return jnp.dot(inner, down_rows, preferred_element_type=jnp.float32)


MESH = pl.DeviceIdType.MESH
Z_ORDER = (2, 3, 1, 0)


def coordinates():
    dp, col = lax.axis_index("dp"), lax.axis_index("exp")
    row_x = dp + 1 - 2 * (dp % 2)
    row_y = (dp + 2) % 4
    row_d = (row_x + 2) % 4
    core = col % 2
    return dp, col, row_x, row_y, row_d, core


def greet(dp, col, row_x, row_y, core):
    barrier = pltpu.get_barrier_semaphore()
    z = col // 2
    partners = [(row_x, col), (row_y, col), (dp, z * 2 + 1 - core)]
    partners += [(dp, ((z + dz) % 4) * 2 + core) for dz in (1, 2, 3)]
    for partner in partners:
        pl.semaphore_signal(barrier, inc=1, device_id=partner, device_id_type=MESH)
    pl.semaphore_wait(barrier, 6)


def spread_kernel(
    own_ref, all_ref, local_sem, z_send, z_recv, x_send, x_recv, y_send, y_recv,
    fx_send, fx_recv, fy_send, fy_recv, c_send, c_recv,
):
    dp, col, row_x, row_y, row_d, core = coordinates()
    z = col // 2
    sibling = z * 2 + 1 - core
    half = own_ref.shape[0] // 2
    greet(dp, col, row_x, row_y, core)

    def remote(src, dst, send, recv, target):
        return pltpu.make_async_remote_copy(
            src_ref=src, dst_ref=dst, send_sem=send, recv_sem=recv,
            device_id=target, device_id_type=MESH,
        )

    started = []

    def go(copy):
        copy.start()
        started.append(copy)
        return copy

    local = pltpu.make_async_copy(own_ref, all_ref.at[dp, col], local_sem)
    local.start()
    z_copies = [None] * 4
    x_copies, y_copies, fx_copies, fy_copies = [], [], [], []

    def column(dz):
        return ((z - dz + 4) % 4) * 2 + core

    def first(dz):
        if dz:
            z_copies[dz].wait_recv()
        where = column(dz)
        src = all_ref.at[dp, where] if dz else own_ref
        dst = all_ref.at[dp, where]
        x_copies.append(go(remote(src, dst, x_send.at[dz], x_recv.at[dz], (row_x, col))))
        y_copies.append(go(remote(src, dst, y_send.at[dz], y_recv.at[dz], (row_y, col))))
        if dz == 0:
            for step in (1, 2, 3):
                target = (dp, ((z + step) % 4) * 2 + core)
                z_copies[step] = go(
                    remote(own_ref, dst, z_send.at[step], z_recv.at[step], target)
                )
        go(remote(src, dst, c_send.at[dz, 0], c_recv.at[dz, 0], (dp, sibling)))

    def second(dz):
        where = column(dz)
        x_copies[dz].wait_recv()
        block = all_ref.at[row_x, where]
        part = all_ref.at[row_x, where, pl.ds(0, half)]
        fy_copies.append(go(remote(part, part, fy_send.at[dz], fy_recv.at[dz], (row_y, col))))
        go(remote(block, block, c_send.at[dz, 1], c_recv.at[dz, 1], (dp, sibling)))
        y_copies[dz].wait_recv()
        block = all_ref.at[row_y, where]
        part = all_ref.at[row_y, where, pl.ds(half, half)]
        fx_copies.append(go(remote(part, part, fx_send.at[dz], fx_recv.at[dz], (row_x, col))))
        go(remote(block, block, c_send.at[dz, 2], c_recv.at[dz, 2], (dp, sibling)))

    def third(dz):
        fy_copies[dz].wait_recv()
        fx_copies[dz].wait_recv()
        block = all_ref.at[row_d, column(dz)]
        go(remote(block, block, c_send.at[dz, 3], c_recv.at[dz, 3], (dp, sibling)))

    for step in range(6):
        if step < 4:
            first(step)
        if 1 <= step < 5:
            second(step - 1)
        if step >= 2:
            third(step - 2)
    local.wait()
    for copy in started:
        copy.wait_send()
    rows = (dp, row_x, row_y, row_d)
    for dz in range(4):
        for k in range(4):
            block = all_ref.at[rows[k], ((z - dz + 4) % 4) * 2 + 1 - core]
            remote(block, block, c_send.at[dz, k], c_recv.at[dz, k], (dp, sibling)).wait_recv()


def spread(normed):
    rows, width = normed.shape
    dma = pltpu.SemaphoreType.DMA
    return pl.pallas_call(
        spread_kernel,
        out_shape=jax.ShapeDtypeStruct((4, 8, rows, width), normed.dtype),
        in_specs=[pl.BlockSpec(memory_space=pl.ANY)],
        out_specs=pl.BlockSpec(memory_space=pl.ANY),
        scratch_shapes=[dma] + [dma((4,))] * 10 + [dma((4, 4))] * 2,
        compiler_params=pltpu.CompilerParams(collective_id=1, has_side_effects=True),
        name="spread_tokens",
    )(normed)


def collect_kernel(
    part_ref, residual_ref, out_ref, acc, from_core, half_x, half_y, full_x, full_y, from_z,
    load_sem, c_send, c_recv, hx_send, hx_recv, hy_send, hy_recv, x_send, x_recv, y_send, y_recv,
    z_send, z_recv,
):
    dp, col, row_x, row_y, row_d, core = coordinates()
    z = col // 2
    sibling = z * 2 + 1 - core
    rows = residual_ref.shape[0]
    half = rows // 2
    chunk = 16
    greet(dp, col, row_x, row_y, core)
    owners = (dp, row_x, row_y, row_d)

    def remote(src, dst, send, recv, target):
        return pltpu.make_async_remote_copy(
            src_ref=src, dst_ref=dst, send_sem=send, recv_sem=recv,
            device_id=target, device_id_type=MESH,
        )

    loads, crossings, started = {}, {}, []
    halves_x, halves_y, fulls_x, fulls_y, z_copies = {}, {}, {}, {}, {}

    def fetch(dz, k):
        column = ((z + dz) % 4) * 2
        crossing = remote(
            part_ref.at[owners[k], column + 1 - core], from_core.at[dz, k],
            c_send.at[dz, k], c_recv.at[dz, k], (dp, sibling),
        )
        crossing.start()
        crossings[dz, k] = crossing
        started.append(crossing)
        load = pltpu.make_async_copy(
            part_ref.at[owners[k], column + core], acc.at[dz, k], load_sem.at[dz, k]
        )
        load.start()
        loads[dz, k] = load

    def go(copy):
        copy.start()
        started.append(copy)
        return copy

    def wide(ref):
        return ref[...].astype(jnp.float32)

    def join(dz, k):
        loads[dz, k].wait()
        crossings[dz, k].wait_recv()

    def add(dz, k, start, size, extras):
        @pl.loop(0, size // chunk)
        def _(i):
            at = pl.ds(pl.multiple_of(start + i * chunk, chunk), chunk)
            total = wide(acc.at[dz, k, at]) + wide(from_core.at[dz, k, at])
            for extra, shift in extras:
                total += wide(extra.at[pl.ds(pl.multiple_of(start - shift + i * chunk, chunk), chunk)])
            acc[dz, k, at] = total.astype(acc.dtype)

    for step in range(6):
        if step < 4:
            fetch(Z_ORDER[step], 3)
        if 1 <= step < 5:
            fetch(Z_ORDER[step - 1], 1)
            fetch(Z_ORDER[step - 1], 2)
        if step >= 2:
            fetch(Z_ORDER[step - 2], 0)

    def first(dz):
        join(dz, 3)
        add(dz, 3, 0, rows, [])
        halves_x[dz] = go(remote(
            acc.at[dz, 3, pl.ds(0, half)], half_x.at[dz], hx_send.at[dz], hx_recv.at[dz], (row_x, col)
        ))
        halves_y[dz] = go(remote(
            acc.at[dz, 3, pl.ds(half, half)], half_y.at[dz], hy_send.at[dz], hy_recv.at[dz], (row_y, col)
        ))

    def second(dz):
        join(dz, 1)
        add(dz, 1, 0, half, [])
        halves_y[dz].wait_recv()
        add(dz, 1, half, half, [(half_y.at[dz], half)])
        fulls_x[dz] = go(remote(acc.at[dz, 1], full_x.at[dz], x_send.at[dz], x_recv.at[dz], (row_x, col)))
        join(dz, 2)
        add(dz, 2, half, half, [])
        halves_x[dz].wait_recv()
        add(dz, 2, 0, half, [(half_x.at[dz], 0)])
        fulls_y[dz] = go(remote(acc.at[dz, 2], full_y.at[dz], y_send.at[dz], y_recv.at[dz], (row_y, col)))

    def third(dz):
        join(dz, 0)
        fulls_x[dz].wait_recv()
        fulls_y[dz].wait_recv()
        if dz:
            add(dz, 0, 0, rows, [(full_x.at[dz], 0), (full_y.at[dz], 0)])
            target = (dp, ((z + dz) % 4) * 2 + core)
            z_copies[dz] = go(remote(
                acc.at[dz, 0], from_z.at[dz - 1], z_send.at[dz - 1], z_recv.at[dz - 1], target
            ))
        else:
            for copy in z_copies.values():
                copy.wait_recv()

            @pl.loop(0, rows // chunk)
            def _(i):
                at = pl.ds(pl.multiple_of(i * chunk, chunk), chunk)
                total = wide(acc.at[0, 0, at]) + wide(from_core.at[0, 0, at])
                total += wide(full_x.at[0, at]) + wide(full_y.at[0, at])
                for k in range(3):
                    total += wide(from_z.at[k, at])
                out_ref[at] = (total + wide(residual_ref.at[at])).astype(out_ref.dtype)

    for step in range(6):
        if step < 4:
            first(Z_ORDER[step])
        if 1 <= step < 5:
            second(Z_ORDER[step - 1])
        if step >= 2:
            third(Z_ORDER[step - 2])
    for copy in started:
        copy.wait_send()


def collect(parts, residual):
    rows, width = residual.shape
    dtype = residual.dtype
    dma = pltpu.SemaphoreType.DMA
    vmem = pl.BlockSpec(memory_space=pltpu.VMEM)
    return pl.pallas_call(
        collect_kernel,
        out_shape=jax.ShapeDtypeStruct((rows, width), dtype),
        in_specs=[pl.BlockSpec(memory_space=pl.ANY), vmem],
        out_specs=vmem,
        scratch_shapes=[
            pltpu.VMEM((4, 4, rows, width), dtype),
            pltpu.VMEM((4, 4, rows, width), dtype),
            pltpu.VMEM((4, rows // 2, width), dtype),
            pltpu.VMEM((4, rows // 2, width), dtype),
            pltpu.VMEM((4, rows, width), dtype),
            pltpu.VMEM((4, rows, width), dtype),
            pltpu.VMEM((3, rows, width), dtype),
        ] + [dma((4, 4))] * 3 + [dma((4,))] * 8 + [dma((3,))] * 2,
        compiler_params=pltpu.CompilerParams(
            collective_id=2, has_side_effects=True, vmem_limit_bytes=48 * 2**20
        ),
        name="collect_sums",
    )(parts, residual)


def experts_kernel(
    col_ref, tokens_ref, route_ref, gate_ref, up_ref, down_ref, sgate_ref, sup_ref, sdown_ref,
    parts_ref, grouped, shared,
):
    step = pl.program_id(0)
    col = col_ref[0]
    local_experts, slots_all, width = grouped.shape
    groups, tok_rows = tokens_ref.shape[0], tokens_ref.shape[2]
    picks = route_ref.shape[2] // 2
    slots = local_experts * CAP
    columns = slots_all // CAP // groups
    last = columns + local_experts

    def match(group, weighted):
        slot_ids = lax.broadcasted_iota(jnp.int32, (slots, tok_rows), 0)
        slot_ids = (slot_ids + col * slots).astype(jnp.float32)
        total = jnp.zeros((slots, tok_rows), jnp.float32)
        for k in range(picks):
            value = route_ref[group, 0, picks + k : picks + k + 1, :] if weighted else 1.0
            total += jnp.where(slot_ids == route_ref[group, 0, k : k + 1, :], value, 0.0)
        return total.astype(jnp.bfloat16)

    def two_layers(rows, gate, up, down):
        gates = lax.dot_general(
            rows, gate, (((1,), (1,)), ((), ())), preferred_element_type=jnp.float32
        )
        ups = lax.dot_general(rows, up, (((1,), (1,)), ((), ())), preferred_element_type=jnp.float32)
        inner = (gates / (1.0 + jnp.exp(-gates)) * ups).astype(jnp.bfloat16)
        return jnp.dot(inner, down, preferred_element_type=jnp.float32).astype(jnp.bfloat16)

    @pl.when(step < columns)
    def _():
        for group in range(groups):
            at = pl.ds(pl.multiple_of((step * groups + group) * CAP, CAP), CAP)
            rows = jnp.dot(
                match(group, False), tokens_ref[group, 0], preferred_element_type=jnp.float32
            ).astype(jnp.bfloat16)
            for e in range(local_experts):
                grouped[e, at, :] = rows[e * CAP : (e + 1) * CAP]

        @pl.when(step == col)
        def _():
            for group in range(groups):
                shared[group * tok_rows : (group + 1) * tok_rows, :] = tokens_ref[group, 0]

    @pl.when((step >= columns) & (step < last))
    def _():
        expert = step - columns
        grouped[expert] = two_layers(grouped[expert], gate_ref[0], up_ref[0], down_ref[0])

    @pl.when(step == last)
    def _():
        shared[...] = two_layers(shared[...], sgate_ref[...], sup_ref[...], sdown_ref[...])

    @pl.when(step > last)
    def _():
        column = step - last - 1
        here = jnp.where(column == col, 1.0, 0.0)
        for group in range(groups):
            at = pl.ds(pl.multiple_of((column * groups + group) * CAP, CAP), CAP)
            rows = jnp.concatenate([grouped[e, at, :] for e in range(local_experts)], axis=0)
            sums = lax.dot_general(
                match(group, True), rows, (((0,), (0,)), ((), ())), preferred_element_type=jnp.float32
            )
            own = shared[group * tok_rows : (group + 1) * tok_rows, :].astype(jnp.float32)
            parts_ref[group, 0] = (sums + here * own).astype(jnp.bfloat16)


def run_experts(tokens, routes, gate, up, down, sgate, sup, sdown):
    groups, columns, tok_rows, width = tokens.shape
    local_experts, units, _ = gate.shape
    route_rows = routes.shape[2]
    last = columns + local_experts
    col = lax.axis_index("exp").astype(jnp.int32).reshape(1)

    def column_in(i, col_ref):
        j = jnp.where(i > last, i - last - 1, jnp.minimum(i, columns - 1))
        return (0, j, 0, 0)

    def tokens_in(i, col_ref):
        return (0, jnp.minimum(i, columns - 1), 0, 0)

    def expert_in(i, col_ref):
        return (jnp.clip(i - columns, 0, local_experts - 1), 0, 0)

    def parts_out(i, col_ref):
        return (0, jnp.clip(i - last - 1, 0, columns - 1), 0, 0)

    def shared_in(i, col_ref):
        return (0, 0)

    once = pl.Buffered(1)
    return pl.pallas_call(
        experts_kernel,
        out_shape=jax.ShapeDtypeStruct(tokens.shape, tokens.dtype),
        grid_spec=pltpu.PrefetchScalarGridSpec(
            num_scalar_prefetch=1,
            grid=(last + 1 + columns,),
            in_specs=[
                pl.BlockSpec((groups, 1, tok_rows, width), tokens_in),
                pl.BlockSpec((groups, 1, route_rows, tok_rows), column_in),
                pl.BlockSpec((1, units, width), expert_in),
                pl.BlockSpec((1, units, width), expert_in),
                pl.BlockSpec((1, units, width), expert_in),
                pl.BlockSpec(sgate.shape, shared_in, pipeline_mode=once),
                pl.BlockSpec(sup.shape, shared_in, pipeline_mode=once),
                pl.BlockSpec(sdown.shape, shared_in, pipeline_mode=once),
            ],
            out_specs=pl.BlockSpec((groups, 1, tok_rows, width), parts_out),
            scratch_shapes=[
                pltpu.VMEM((local_experts, columns * groups * CAP, width), jnp.bfloat16),
                pltpu.VMEM((groups * tok_rows, width), jnp.bfloat16),
            ],
        ),
        compiler_params=pltpu.CompilerParams(
            dimension_semantics=("arbitrary",), vmem_limit_bytes=60 * 2**20
        ),
        name="experts",
    )(col, tokens, routes, gate, up, down, sgate, sup, sdown)


def on_device(
    hidden,
    queries,
    draft_entries,
    key_pool,
    value_pool,
    page_table,
    cache_len,
    parents,
    out_proj,
    norm_gain,
    expert_gate,
    expert_up,
    expert_down,
    shared_gate,
    shared_up,
    shared_down,
    expert_ids,
    expert_weights,
):
    tok_rows, model_width = hidden.shape
    local_experts = expert_gate.shape[0]
    column_count = lax.axis_size("exp")
    expert_count = local_experts * column_count
    pick_count = expert_ids.shape[1]
    flat_experts = expert_ids.reshape(-1)
    onehot = (flat_experts[:, None] == jnp.arange(expert_count, dtype=jnp.int32)[None, :]).astype(
        jnp.int32
    )
    slot_ids = jnp.sum((jnp.cumsum(onehot, axis=0) - 1) * onehot, axis=1)
    destinations = flat_experts * CAP + slot_ids
    small_slice = column_count == 8 and lax.axis_size("dp") == 4
    if small_slice:
        route = jnp.concatenate(
            [destinations.reshape(tok_rows, pick_count).astype(jnp.float32), expert_weights], axis=1
        ).T
        routes = lax.all_gather(route, ("dp", "exp")).reshape(4, 8, 2 * pick_count, tok_rows)
    local_requests, draft_nodes = parents.shape
    group_size = HEADS // KVH
    query_heads = queries.reshape(local_requests, draft_nodes, KVH, group_size, HD)
    draft_keys = draft_entries[0].reshape(local_requests, draft_nodes, KVH, HD)
    draft_values = draft_entries[1].reshape(local_requests, draft_nodes, KVH, HD)
    reached = tree_reach(parents)
    tree_scores, tree_mask = score_block(query_heads, draft_keys, reached > 0.5)
    tree_state = fold_keys(
        blank_state(local_requests, draft_nodes, KVH, group_size, HD),
        tree_scores,
        tree_mask,
        draft_values,
    )
    final_top, final_total, final_sum = pool_state(
        tree_state,
        query_heads,
        page_table,
        cache_len,
        (
            lax.all_gather(key_pool, "dp", axis=0, tiled=True),
            lax.all_gather(value_pool, "dp", axis=0, tiled=True),
        ),
    )
    attention = (
        (final_sum / jnp.transpose(final_total, (0, 3, 1, 2))[..., None])
        .reshape(tok_rows, queries.shape[1])
        .astype(jnp.bfloat16)
    )
    residual = (
        hidden.astype(jnp.float32)
        + jnp.dot(attention, out_proj, preferred_element_type=jnp.float32)
    ).astype(jnp.bfloat16)
    residual_wide = residual.astype(jnp.float32)
    scale_rows = lax.rsqrt(
        jnp.mean(residual_wide * residual_wide, axis=-1, keepdims=True) + NORM_EPSILON
    )
    normed = (residual_wide * scale_rows * norm_gain.astype(jnp.float32)).astype(jnp.bfloat16)
    if small_slice:
        parts = run_experts(
            spread(normed), routes, expert_gate, expert_up, expert_down, shared_gate, shared_up, shared_down
        )
        return collect(parts, residual)
    token_rows = jnp.arange(tok_rows * pick_count, dtype=jnp.int32) // pick_count
    outgoing = (
        jnp.zeros((expert_count * CAP, model_width), jnp.bfloat16)
        .at[destinations]
        .set(normed[token_rows])
    )
    outgoing = outgoing.reshape(column_count, local_experts, CAP, model_width)
    arrived = lax.all_to_all(outgoing, "exp", split_axis=0, concat_axis=0, tiled=True)
    grouped, group_tokens = (
        lax.all_gather(arrived, "dp", axis=0, tiled=True),
        lax.all_gather(normed, "dp", axis=0, tiled=True),
    )
    routed_terms = expert_block(grouped, expert_gate, expert_up, expert_down)
    shared_terms = shared_block(group_tokens, shared_gate, shared_up, shared_down)
    routed_sum, shared_sum = (
        lax.psum_scatter(
            routed_terms.astype(jnp.bfloat16), "dp", scatter_dimension=0, tiled=True
        ).astype(jnp.float32),
        lax.psum_scatter(
            shared_terms.astype(jnp.bfloat16), "dp", scatter_dimension=0, tiled=True
        ).astype(jnp.float32),
    )
    returned = lax.all_to_all(
        routed_sum.astype(jnp.bfloat16), "exp", split_axis=0, concat_axis=0, tiled=True
    )
    returned_rows = returned.reshape(expert_count * CAP, model_width)
    picked_rows = (
        returned_rows[destinations].astype(jnp.float32).reshape(tok_rows, pick_count, model_width)
    )
    routed_out = jnp.sum(picked_rows * expert_weights[:, :, None], axis=1)
    return (residual.astype(jnp.float32) + routed_out + shared_sum).astype(jnp.bfloat16)


def solution(mesh):
    placed = (
        P(("dp", "exp"), None),
        P(("dp", "exp"), None),
        P(None, ("dp", "exp"), None),
        P(("dp", "exp"), None, None),
        P(("dp", "exp"), None, None),
        P(("dp", "exp"), None),
        P(("dp", "exp")),
        P(("dp", "exp"), None),
        P(),
        P(),
        P("exp", "dp", None),
        P("exp", "dp", None),
        P("exp", "dp", None),
        P("dp", None),
        P("dp", None),
        P("dp", None),
        P(("dp", "exp"), None),
        P(("dp", "exp"), None),
    )
    return jax.shard_map(
        on_device, mesh=mesh, in_specs=placed, out_specs=P(("dp", "exp"), None), check_vma=False
    )
```

```python
import jax
import jax.numpy as jnp
from jax import lax
from jax.experimental import pallas as pl
from jax.experimental.pallas import tpu as pltpu
from jax.sharding import PartitionSpec as P

HEADS = 16
KVH = 4
HD = 128
CAP = 16


NEG_FILL = -1e30
NORM_EPSILON = 1e-06
HIGHEST_PRECISION = lax.Precision.HIGHEST


def tree_reach(parents):
    node_count = parents.shape[-1]
    node_index = jnp.arange(node_count, dtype=jnp.int32)
    linked = (parents[:, :, None] == node_index[None, None, :]).astype(jnp.float32)
    reached = jnp.minimum(linked + jnp.eye(node_count, dtype=jnp.float32)[None], 1.0)
    for rounds in range(max(1, (node_count - 1).bit_length())):
        reached = jnp.minimum(
            jnp.einsum("rij,rjk->rik", reached, reached, precision=HIGHEST_PRECISION), 1.0
        )
    return reached


def score_block(query_heads, key_rows, live_mask):
    raw_scores = jnp.einsum(
        "rtgnd,rcgd->rgntc", query_heads, key_rows, preferred_element_type=jnp.float32
    ) * key_rows.shape[-1] ** (-0.5)
    wide_mask = live_mask[:, None, None]
    return (jnp.where(wide_mask, raw_scores, NEG_FILL), wide_mask)


def fold_keys(carry_state, scores, wide_mask, value_rows):
    running_top, running_total, running_sum = carry_state
    fresh_top = jnp.maximum(running_top, jnp.max(scores, axis=-1))
    rescale = jnp.exp(running_top - fresh_top)
    exponents = jnp.where(wide_mask, jnp.exp(scores - fresh_top[..., None]), 0.0)
    weights = exponents.astype(jnp.bfloat16)
    new_total = running_total * rescale + jnp.sum(exponents, axis=-1)
    mixed = jnp.einsum("rgntc,rcgd->rtgnd", weights, value_rows, preferred_element_type=jnp.float32)
    new_sum = running_sum * jnp.transpose(rescale, (0, 3, 1, 2))[..., None] + mixed
    return (fresh_top, new_total, new_sum)


def pool_state(carry_state, query_heads, table_rows, lengths, pieces):
    piece_keys, piece_values = pieces
    piece_count = piece_keys.shape[0]
    request_count, pages_per = table_rows.shape
    page_size = piece_keys.shape[1]
    key_heads = query_heads.shape[2]
    inside = (table_rows >= 0) & (table_rows < piece_count)
    picked = jnp.clip(table_rows, 0, piece_count - 1)
    cache_keys = piece_keys[picked].reshape(request_count, pages_per * page_size, key_heads, -1)
    cache_values = piece_values[picked].reshape(request_count, pages_per * page_size, key_heads, -1)
    positions = jnp.arange(pages_per * page_size, dtype=jnp.int32)
    usable = jnp.repeat(inside, page_size, axis=1) & (positions[None, :] < lengths[:, None])
    live_mask = jnp.broadcast_to(
        usable[:, None, :], (request_count, query_heads.shape[1], pages_per * page_size)
    )
    scores, wide_mask = score_block(query_heads, cache_keys, live_mask)
    return fold_keys(carry_state, scores, wide_mask, cache_values)


def blank_state(request_count, draft_nodes, key_heads, group_size, head_size):
    return (
        jnp.full((request_count, key_heads, group_size, draft_nodes), NEG_FILL, jnp.float32),
        jnp.zeros((request_count, key_heads, group_size, draft_nodes), jnp.float32),
        jnp.zeros((request_count, draft_nodes, key_heads, group_size, head_size), jnp.float32),
    )


def expert_block(grouped, gate_rows, upper_rows, down_rows):
    gate_values = jnp.einsum(
        "sekd,efd->sekf", grouped, gate_rows, preferred_element_type=jnp.float32
    )
    upper_values = jnp.einsum(
        "sekd,efd->sekf", grouped, upper_rows, preferred_element_type=jnp.float32
    )
    inner = (jax.nn.silu(gate_values) * upper_values).astype(jnp.bfloat16)
    return jnp.einsum("sekf,efd->sekd", inner, down_rows, preferred_element_type=jnp.float32)


def shared_block(tokens, gate_rows, upper_rows, down_rows):
    gate_values = jnp.einsum("td,fd->tf", tokens, gate_rows, preferred_element_type=jnp.float32)
    upper_values = jnp.einsum("td,fd->tf", tokens, upper_rows, preferred_element_type=jnp.float32)
    inner = (jax.nn.silu(gate_values) * upper_values).astype(jnp.bfloat16)
    return jnp.dot(inner, down_rows, preferred_element_type=jnp.float32)


MESH = pl.DeviceIdType.MESH
Z_ORDER = (2, 3, 1, 0)


def coordinates():
    dp, col = lax.axis_index("dp"), lax.axis_index("exp")
    row_x = dp + 1 - 2 * (dp % 2)
    row_y = (dp + 2) % 4
    row_d = (row_x + 2) % 4
    core = col % 2
    return dp, col, row_x, row_y, row_d, core


def greet(dp, col, row_x, row_y, core):
    barrier = pltpu.get_barrier_semaphore()
    z = col // 2
    partners = [(row_x, col), (row_y, col), (dp, z * 2 + 1 - core)]
    partners += [(dp, ((z + dz) % 4) * 2 + core) for dz in (1, 2, 3)]
    for partner in partners:
        pl.semaphore_signal(barrier, inc=1, device_id=partner, device_id_type=MESH)
    pl.semaphore_wait(barrier, 6)


def spread_kernel(own_ref, all_ref, *sems):
    dp, col, row_x, row_y, row_d, core = coordinates()
    greet(dp, col, row_x, row_y, core)
    spread_block(own_ref, all_ref, *sems)


def pages_kernel(
    route_ref, key_ref, value_ref, routes_ref, keys_ref, values_ref, load_sem, x_send, x_recv,
    y_send, y_recv, fx_send, fx_recv, fy_send, fy_recv, *sems,
):
    dp, col, row_x, row_y, row_d, core = coordinates()
    half = key_ref.shape[0] // 2
    greet(dp, col, row_x, row_y, core)

    def send(src, dst, send_sem, recv_sem, row):
        copy = pltpu.make_async_remote_copy(
            src_ref=src, dst_ref=dst, send_sem=send_sem, recv_sem=recv_sem,
            device_id=(row, col), device_id_type=MESH,
        )
        copy.start()
        return copy

    pools = ((key_ref, keys_ref), (value_ref, values_ref))
    to_x, to_y, on_x, on_y, local = [], [], [], [], []
    for i, (own, pool) in enumerate(pools):
        to_x.append(send(own, pool.at[dp], x_send.at[i], x_recv.at[i], row_x))
        to_y.append(send(own, pool.at[dp], y_send.at[i], y_recv.at[i], row_y))
    for i, (own, pool) in enumerate(pools):
        local.append(pltpu.make_async_copy(own, pool.at[dp], load_sem.at[i]))
        local[i].start()
    for i, (own, pool) in enumerate(pools):
        to_x[i].wait_recv()
        part = pool.at[row_x, pl.ds(0, half)]
        on_y.append(send(part, part, fy_send.at[i], fy_recv.at[i], row_y))
        to_y[i].wait_recv()
        part = pool.at[row_y, pl.ds(half, half)]
        on_x.append(send(part, part, fx_send.at[i], fx_recv.at[i], row_x))
    spread_block(route_ref, routes_ref, *sems)
    for i in range(2):
        local[i].wait()
        to_x[i].wait_send()
        to_y[i].wait_send()
        on_x[i].wait()
        on_y[i].wait()


def share_pages(route, keys, values):
    dma = pltpu.SemaphoreType.DMA
    anywhere = pl.BlockSpec(memory_space=pl.ANY)
    pool = jax.ShapeDtypeStruct((4,) + keys.shape, keys.dtype)
    return pl.pallas_call(
        pages_kernel,
        out_shape=[jax.ShapeDtypeStruct((4, 8) + route.shape, route.dtype), pool, pool],
        in_specs=[anywhere] * 3,
        out_specs=[anywhere] * 3,
        scratch_shapes=[dma((2,))] * 9 + [dma] + [dma((4,))] * 10 + [dma((4, 4))] * 2,
        compiler_params=pltpu.CompilerParams(collective_id=3, has_side_effects=True),
        name="share_pages",
    )(route, keys, values)


def spread_block(
    own_ref, all_ref, local_sem, z_send, z_recv, x_send, x_recv, y_send, y_recv,
    fx_send, fx_recv, fy_send, fy_recv, c_send, c_recv,
):
    dp, col, row_x, row_y, row_d, core = coordinates()
    z = col // 2
    sibling = z * 2 + 1 - core
    half = own_ref.shape[0] // 2

    def remote(src, dst, send, recv, target):
        return pltpu.make_async_remote_copy(
            src_ref=src, dst_ref=dst, send_sem=send, recv_sem=recv,
            device_id=target, device_id_type=MESH,
        )

    started = []

    def go(copy):
        copy.start()
        started.append(copy)
        return copy

    local = pltpu.make_async_copy(own_ref, all_ref.at[dp, col], local_sem)
    local.start()
    z_copies = [None] * 4
    x_copies, y_copies, fx_copies, fy_copies = [], [], [], []

    def column(dz):
        return ((z - dz + 4) % 4) * 2 + core

    def first(dz):
        if dz:
            z_copies[dz].wait_recv()
        where = column(dz)
        src = all_ref.at[dp, where] if dz else own_ref
        dst = all_ref.at[dp, where]
        x_copies.append(go(remote(src, dst, x_send.at[dz], x_recv.at[dz], (row_x, col))))
        y_copies.append(go(remote(src, dst, y_send.at[dz], y_recv.at[dz], (row_y, col))))
        if dz == 0:
            for step in (1, 2, 3):
                target = (dp, ((z + step) % 4) * 2 + core)
                z_copies[step] = go(
                    remote(own_ref, dst, z_send.at[step], z_recv.at[step], target)
                )
        go(remote(src, dst, c_send.at[dz, 0], c_recv.at[dz, 0], (dp, sibling)))

    def second(dz):
        where = column(dz)
        x_copies[dz].wait_recv()
        block = all_ref.at[row_x, where]
        part = all_ref.at[row_x, where, pl.ds(0, half)]
        fy_copies.append(go(remote(part, part, fy_send.at[dz], fy_recv.at[dz], (row_y, col))))
        go(remote(block, block, c_send.at[dz, 1], c_recv.at[dz, 1], (dp, sibling)))
        y_copies[dz].wait_recv()
        block = all_ref.at[row_y, where]
        part = all_ref.at[row_y, where, pl.ds(half, half)]
        fx_copies.append(go(remote(part, part, fx_send.at[dz], fx_recv.at[dz], (row_x, col))))
        go(remote(block, block, c_send.at[dz, 2], c_recv.at[dz, 2], (dp, sibling)))

    def third(dz):
        fy_copies[dz].wait_recv()
        fx_copies[dz].wait_recv()
        block = all_ref.at[row_d, column(dz)]
        go(remote(block, block, c_send.at[dz, 3], c_recv.at[dz, 3], (dp, sibling)))

    for step in range(6):
        if step < 4:
            first(step)
        if 1 <= step < 5:
            second(step - 1)
        if step >= 2:
            third(step - 2)
    local.wait()
    for copy in started:
        copy.wait_send()
    rows = (dp, row_x, row_y, row_d)
    for dz in range(4):
        for k in range(4):
            block = all_ref.at[rows[k], ((z - dz + 4) % 4) * 2 + 1 - core]
            remote(block, block, c_send.at[dz, k], c_recv.at[dz, k], (dp, sibling)).wait_recv()


def spread(normed):
    rows, width = normed.shape
    dma = pltpu.SemaphoreType.DMA
    return pl.pallas_call(
        spread_kernel,
        out_shape=jax.ShapeDtypeStruct((4, 8, rows, width), normed.dtype),
        in_specs=[pl.BlockSpec(memory_space=pl.ANY)],
        out_specs=pl.BlockSpec(memory_space=pl.ANY),
        scratch_shapes=[dma] + [dma((4,))] * 10 + [dma((4, 4))] * 2,
        compiler_params=pltpu.CompilerParams(collective_id=1, has_side_effects=True),
        name="spread_tokens",
    )(normed)


def collect_kernel(
    part_ref, residual_ref, out_ref, acc, from_core, half_x, half_y, full_x, full_y, from_z,
    load_sem, c_send, c_recv, hx_send, hx_recv, hy_send, hy_recv, x_send, x_recv, y_send, y_recv,
    z_send, z_recv,
):
    dp, col, row_x, row_y, row_d, core = coordinates()
    z = col // 2
    sibling = z * 2 + 1 - core
    rows = residual_ref.shape[0]
    half = rows // 2
    chunk = 16
    greet(dp, col, row_x, row_y, core)
    owners = (dp, row_x, row_y, row_d)

    def remote(src, dst, send, recv, target):
        return pltpu.make_async_remote_copy(
            src_ref=src, dst_ref=dst, send_sem=send, recv_sem=recv,
            device_id=target, device_id_type=MESH,
        )

    loads, crossings, started = {}, {}, []
    halves_x, halves_y, fulls_x, fulls_y, z_copies = {}, {}, {}, {}, {}

    def fetch(dz, k):
        column = ((z + dz) % 4) * 2
        crossing = remote(
            part_ref.at[owners[k], column + 1 - core], from_core.at[dz, k],
            c_send.at[dz, k], c_recv.at[dz, k], (dp, sibling),
        )
        crossing.start()
        crossings[dz, k] = crossing
        started.append(crossing)
        load = pltpu.make_async_copy(
            part_ref.at[owners[k], column + core], acc.at[dz, k], load_sem.at[dz, k]
        )
        load.start()
        loads[dz, k] = load

    def go(copy):
        copy.start()
        started.append(copy)
        return copy

    def wide(ref):
        return ref[...].astype(jnp.float32)

    def join(dz, k):
        loads[dz, k].wait()
        crossings[dz, k].wait_recv()

    def add(dz, k, start, size, extras):
        @pl.loop(0, size // chunk)
        def _(i):
            at = pl.ds(pl.multiple_of(start + i * chunk, chunk), chunk)
            total = wide(acc.at[dz, k, at]) + wide(from_core.at[dz, k, at])
            for extra, shift in extras:
                total += wide(extra.at[pl.ds(pl.multiple_of(start - shift + i * chunk, chunk), chunk)])
            acc[dz, k, at] = total.astype(acc.dtype)

    for step in range(6):
        if step < 4:
            fetch(Z_ORDER[step], 3)
        if 1 <= step < 5:
            fetch(Z_ORDER[step - 1], 1)
            fetch(Z_ORDER[step - 1], 2)
        if step >= 2:
            fetch(Z_ORDER[step - 2], 0)

    def first(dz):
        join(dz, 3)
        add(dz, 3, 0, rows, [])
        halves_x[dz] = go(remote(
            acc.at[dz, 3, pl.ds(0, half)], half_x.at[dz], hx_send.at[dz], hx_recv.at[dz], (row_x, col)
        ))
        halves_y[dz] = go(remote(
            acc.at[dz, 3, pl.ds(half, half)], half_y.at[dz], hy_send.at[dz], hy_recv.at[dz], (row_y, col)
        ))

    def second(dz):
        join(dz, 1)
        add(dz, 1, 0, half, [])
        halves_y[dz].wait_recv()
        add(dz, 1, half, half, [(half_y.at[dz], half)])
        fulls_x[dz] = go(remote(acc.at[dz, 1], full_x.at[dz], x_send.at[dz], x_recv.at[dz], (row_x, col)))
        join(dz, 2)
        add(dz, 2, half, half, [])
        halves_x[dz].wait_recv()
        add(dz, 2, 0, half, [(half_x.at[dz], 0)])
        fulls_y[dz] = go(remote(acc.at[dz, 2], full_y.at[dz], y_send.at[dz], y_recv.at[dz], (row_y, col)))

    def third(dz):
        join(dz, 0)
        fulls_x[dz].wait_recv()
        fulls_y[dz].wait_recv()
        if dz:
            add(dz, 0, 0, rows, [(full_x.at[dz], 0), (full_y.at[dz], 0)])
            target = (dp, ((z + dz) % 4) * 2 + core)
            z_copies[dz] = go(remote(
                acc.at[dz, 0], from_z.at[dz - 1], z_send.at[dz - 1], z_recv.at[dz - 1], target
            ))
        else:
            for copy in z_copies.values():
                copy.wait_recv()

            @pl.loop(0, rows // chunk)
            def _(i):
                at = pl.ds(pl.multiple_of(i * chunk, chunk), chunk)
                total = wide(acc.at[0, 0, at]) + wide(from_core.at[0, 0, at])
                total += wide(full_x.at[0, at]) + wide(full_y.at[0, at])
                for k in range(3):
                    total += wide(from_z.at[k, at])
                out_ref[at] = (total + wide(residual_ref.at[at])).astype(out_ref.dtype)

    for step in range(6):
        if step < 4:
            first(Z_ORDER[step])
        if 1 <= step < 5:
            second(Z_ORDER[step - 1])
        if step >= 2:
            third(Z_ORDER[step - 2])
    for copy in started:
        copy.wait_send()


def collect(parts, residual):
    rows, width = residual.shape
    dtype = residual.dtype
    dma = pltpu.SemaphoreType.DMA
    vmem = pl.BlockSpec(memory_space=pltpu.VMEM)
    return pl.pallas_call(
        collect_kernel,
        out_shape=jax.ShapeDtypeStruct((rows, width), dtype),
        in_specs=[pl.BlockSpec(memory_space=pl.ANY), vmem],
        out_specs=vmem,
        scratch_shapes=[
            pltpu.VMEM((4, 4, rows, width), dtype),
            pltpu.VMEM((4, 4, rows, width), dtype),
            pltpu.VMEM((4, rows // 2, width), dtype),
            pltpu.VMEM((4, rows // 2, width), dtype),
            pltpu.VMEM((4, rows, width), dtype),
            pltpu.VMEM((4, rows, width), dtype),
            pltpu.VMEM((3, rows, width), dtype),
        ] + [dma((4, 4))] * 3 + [dma((4,))] * 8 + [dma((3,))] * 2,
        compiler_params=pltpu.CompilerParams(
            collective_id=2, has_side_effects=True, vmem_limit_bytes=48 * 2**20
        ),
        name="collect_sums",
    )(parts, residual)


def experts_kernel(
    col_ref, tokens_ref, route_ref, gate_ref, up_ref, down_ref, sgate_ref, sup_ref, sdown_ref,
    parts_ref, grouped, shared, joined,
):
    step = pl.program_id(0)
    col = col_ref[0]
    local_experts, slots_all, width = grouped.shape
    groups, tok_rows = tokens_ref.shape[0], tokens_ref.shape[2]
    picks = route_ref.shape[2] // 2
    slots = local_experts * CAP
    columns = slots_all // CAP // groups
    last = columns + local_experts

    def match(group, weighted):
        slot_ids = lax.broadcasted_iota(jnp.int32, (slots, tok_rows), 0)
        slot_ids = (slot_ids + col * slots).astype(jnp.float32)
        total = jnp.zeros((slots, tok_rows), jnp.float32)
        for k in range(picks):
            value = route_ref[group, 0, picks + k : picks + k + 1, :] if weighted else 1.0
            total += jnp.where(slot_ids == route_ref[group, 0, k : k + 1, :], value, 0.0)
        return total.astype(jnp.bfloat16)

    def two_layers(rows, gate, up, down):
        units = gate.shape[0]
        offset = joined.shape[0] - units
        joined[0:units, :] = gate
        joined[offset : offset + units, :] = up
        both = lax.dot_general(
            rows, joined[...], (((1,), (1,)), ((), ())), preferred_element_type=jnp.float32
        )
        gates, ups = both[:, 0:units], both[:, offset : offset + units]
        inner = (gates / (1.0 + jnp.exp(-gates)) * ups).astype(jnp.bfloat16)
        return jnp.dot(inner, down, preferred_element_type=jnp.float32).astype(jnp.bfloat16)

    @pl.when(step < columns)
    def _():
        for group in range(groups):
            at = pl.ds(pl.multiple_of((step * groups + group) * CAP, CAP), CAP)
            rows = jnp.dot(
                match(group, False), tokens_ref[group, 0], preferred_element_type=jnp.float32
            ).astype(jnp.bfloat16)
            for e in range(local_experts):
                grouped[e, at, :] = rows[e * CAP : (e + 1) * CAP]

        @pl.when(step == col)
        def _():
            for group in range(groups):
                shared[group * tok_rows : (group + 1) * tok_rows, :] = tokens_ref[group, 0]

    @pl.when((step >= columns) & (step < last))
    def _():
        expert = step - columns
        grouped[expert] = two_layers(grouped[expert], gate_ref[0], up_ref[0], down_ref[0])

    @pl.when(step == last)
    def _():
        shared[...] = two_layers(shared[...], sgate_ref[...], sup_ref[...], sdown_ref[...])

    @pl.when(step > last)
    def _():
        column = step - last - 1
        here = jnp.where(column == col, 1.0, 0.0)
        for group in range(groups):
            at = pl.ds(pl.multiple_of((column * groups + group) * CAP, CAP), CAP)
            rows = jnp.concatenate([grouped[e, at, :] for e in range(local_experts)], axis=0)
            sums = lax.dot_general(
                match(group, True), rows, (((0,), (0,)), ((), ())), preferred_element_type=jnp.float32
            )
            own = shared[group * tok_rows : (group + 1) * tok_rows, :].astype(jnp.float32)
            parts_ref[group, 0] = (sums + here * own).astype(jnp.bfloat16)


def run_experts(tokens, routes, gate, up, down, sgate, sup, sdown):
    groups, columns, tok_rows, width = tokens.shape
    local_experts, units, _ = gate.shape
    route_rows = routes.shape[2]
    last = columns + local_experts
    col = lax.axis_index("exp").astype(jnp.int32).reshape(1)

    def column_in(i, col_ref):
        j = jnp.where(i > last, i - last - 1, jnp.minimum(i, columns - 1))
        return (0, j, 0, 0)

    def tokens_in(i, col_ref):
        return (0, jnp.minimum(i, columns - 1), 0, 0)

    def expert_in(i, col_ref):
        return (jnp.clip(i - columns, 0, local_experts - 1), 0, 0)

    def parts_out(i, col_ref):
        return (0, jnp.clip(i - last - 1, 0, columns - 1), 0, 0)

    def shared_in(i, col_ref):
        return (0, 0)

    once = pl.Buffered(1)
    return pl.pallas_call(
        experts_kernel,
        out_shape=jax.ShapeDtypeStruct(tokens.shape, tokens.dtype),
        grid_spec=pltpu.PrefetchScalarGridSpec(
            num_scalar_prefetch=1,
            grid=(last + 1 + columns,),
            in_specs=[
                pl.BlockSpec((groups, 1, tok_rows, width), tokens_in),
                pl.BlockSpec((groups, 1, route_rows, tok_rows), column_in),
                pl.BlockSpec((1, units, width), expert_in),
                pl.BlockSpec((1, units, width), expert_in),
                pl.BlockSpec((1, units, width), expert_in),
                pl.BlockSpec(sgate.shape, shared_in, pipeline_mode=once),
                pl.BlockSpec(sup.shape, shared_in, pipeline_mode=once),
                pl.BlockSpec(sdown.shape, shared_in, pipeline_mode=once),
            ],
            out_specs=pl.BlockSpec((groups, 1, tok_rows, width), parts_out),
            scratch_shapes=[
                pltpu.VMEM((local_experts, columns * groups * CAP, width), jnp.bfloat16),
                pltpu.VMEM((groups * tok_rows, width), jnp.bfloat16),
                pltpu.VMEM((-(-units // 128) * 128 + units, width), jnp.bfloat16),
            ],
        ),
        compiler_params=pltpu.CompilerParams(
            dimension_semantics=("arbitrary",), vmem_limit_bytes=60 * 2**20
        ),
        name="experts",
    )(col, tokens, routes, gate, up, down, sgate, sup, sdown)


def on_device(
    hidden,
    queries,
    draft_entries,
    key_pool,
    value_pool,
    page_table,
    cache_len,
    parents,
    out_proj,
    norm_gain,
    expert_gate,
    expert_up,
    expert_down,
    shared_gate,
    shared_up,
    shared_down,
    expert_ids,
    expert_weights,
):
    tok_rows, model_width = hidden.shape
    local_experts = expert_gate.shape[0]
    column_count = lax.axis_size("exp")
    expert_count = local_experts * column_count
    pick_count = expert_ids.shape[1]
    flat_experts = expert_ids.reshape(-1)
    onehot = (flat_experts[:, None] == jnp.arange(expert_count, dtype=jnp.int32)[None, :]).astype(
        jnp.int32
    )
    slot_ids = jnp.sum((jnp.cumsum(onehot, axis=0) - 1) * onehot, axis=1)
    destinations = flat_experts * CAP + slot_ids
    small_slice = column_count == 8 and lax.axis_size("dp") == 4
    if small_slice:
        spare = -pick_count % 8
        places = destinations.reshape(tok_rows, pick_count).astype(jnp.float32).T
        route = jnp.concatenate(
            [
                jnp.pad(places, ((0, spare), (0, 0)), constant_values=-1.0),
                jnp.pad(expert_weights.T, ((0, spare), (0, 0))),
            ],
            axis=0,
        )
        routes, all_keys, all_values = share_pages(route, key_pool, value_pool)
        all_keys = all_keys.reshape((-1,) + key_pool.shape[1:])
        all_values = all_values.reshape((-1,) + value_pool.shape[1:])
    else:
        all_keys = lax.all_gather(key_pool, "dp", axis=0, tiled=True)
        all_values = lax.all_gather(value_pool, "dp", axis=0, tiled=True)
    local_requests, draft_nodes = parents.shape
    group_size = HEADS // KVH
    query_heads = queries.reshape(local_requests, draft_nodes, KVH, group_size, HD)
    draft_keys = draft_entries[0].reshape(local_requests, draft_nodes, KVH, HD)
    draft_values = draft_entries[1].reshape(local_requests, draft_nodes, KVH, HD)
    reached = tree_reach(parents)
    tree_scores, tree_mask = score_block(query_heads, draft_keys, reached > 0.5)
    tree_state = fold_keys(
        blank_state(local_requests, draft_nodes, KVH, group_size, HD),
        tree_scores,
        tree_mask,
        draft_values,
    )
    final_top, final_total, final_sum = pool_state(
        tree_state,
        query_heads,
        page_table,
        cache_len,
        (all_keys, all_values),
    )
    attention = (
        (final_sum / jnp.transpose(final_total, (0, 3, 1, 2))[..., None])
        .reshape(tok_rows, queries.shape[1])
        .astype(jnp.bfloat16)
    )
    residual = (
        hidden.astype(jnp.float32)
        + jnp.dot(attention, out_proj, preferred_element_type=jnp.float32)
    ).astype(jnp.bfloat16)
    residual_wide = residual.astype(jnp.float32)
    scale_rows = lax.rsqrt(
        jnp.mean(residual_wide * residual_wide, axis=-1, keepdims=True) + NORM_EPSILON
    )
    normed = (residual_wide * scale_rows * norm_gain.astype(jnp.float32)).astype(jnp.bfloat16)
    if small_slice:
        parts = run_experts(
            spread(normed), routes, expert_gate, expert_up, expert_down, shared_gate, shared_up, shared_down
        )
        return collect(parts, residual)
    token_rows = jnp.arange(tok_rows * pick_count, dtype=jnp.int32) // pick_count
    outgoing = (
        jnp.zeros((expert_count * CAP, model_width), jnp.bfloat16)
        .at[destinations]
        .set(normed[token_rows])
    )
    outgoing = outgoing.reshape(column_count, local_experts, CAP, model_width)
    arrived = lax.all_to_all(outgoing, "exp", split_axis=0, concat_axis=0, tiled=True)
    grouped, group_tokens = (
        lax.all_gather(arrived, "dp", axis=0, tiled=True),
        lax.all_gather(normed, "dp", axis=0, tiled=True),
    )
    routed_terms = expert_block(grouped, expert_gate, expert_up, expert_down)
    shared_terms = shared_block(group_tokens, shared_gate, shared_up, shared_down)
    routed_sum, shared_sum = (
        lax.psum_scatter(
            routed_terms.astype(jnp.bfloat16), "dp", scatter_dimension=0, tiled=True
        ).astype(jnp.float32),
        lax.psum_scatter(
            shared_terms.astype(jnp.bfloat16), "dp", scatter_dimension=0, tiled=True
        ).astype(jnp.float32),
    )
    returned = lax.all_to_all(
        routed_sum.astype(jnp.bfloat16), "exp", split_axis=0, concat_axis=0, tiled=True
    )
    returned_rows = returned.reshape(expert_count * CAP, model_width)
    picked_rows = (
        returned_rows[destinations].astype(jnp.float32).reshape(tok_rows, pick_count, model_width)
    )
    routed_out = jnp.sum(picked_rows * expert_weights[:, :, None], axis=1)
    return (residual.astype(jnp.float32) + routed_out + shared_sum).astype(jnp.bfloat16)


def solution(mesh):
    placed = (
        P(("dp", "exp"), None),
        P(("dp", "exp"), None),
        P(None, ("dp", "exp"), None),
        P(("dp", "exp"), None, None),
        P(("dp", "exp"), None, None),
        P(("dp", "exp"), None),
        P(("dp", "exp")),
        P(("dp", "exp"), None),
        P(),
        P(),
        P("exp", "dp", None),
        P("exp", "dp", None),
        P("exp", "dp", None),
        P("dp", None),
        P("dp", None),
        P("dp", None),
        P(("dp", "exp"), None),
        P(("dp", "exp"), None),
    )
    return jax.shard_map(
        on_device, mesh=mesh, in_specs=placed, out_specs=P(("dp", "exp"), None), check_vma=False
    )
```
